32 devices in a mesh: groups: 2 (over y), expert: 8 (over z, core), dp: 2 (over x).
Axes of the slice: x: 2, y: 2, z: 4, core: 2. Of those that a mesh axis runs over, the one named last changes fastest.
Arguments:
- tokens: bfloat16 [4096, 2048], P(('groups', 'expert', 'dp')), parts along dimension 0, may hold values from -6 to 6
- out_grads: bfloat16 [4096, 2048], P(('groups', 'expert', 'dp')), parts along dimension 0, may hold values from -3 to 3
- routes: int32 [4096, 8], P(('groups', 'expert', 'dp')), parts along dimension 0, may hold values from 0 to 15, all different within a row; in each aligned block of 128 rows (0 to 127, 128 to 255, ...) at most 72 rows name the same one
- gates: bfloat16 [4096, 8], P(('groups', 'expert', 'dp')), parts along dimension 0, may hold values from 0.049804688 to 0.5
- gate_weight: bfloat16 [16, 2048, 384], P('expert'), may hold values from -0.125 to 0.125
- up_weight: bfloat16 [16, 2048, 384], P('expert'), may hold values from -0.125 to 0.125
- down_weight: bfloat16 [16, 384, 2048], P('expert'), may hold values from -0.3125 to 0.3125
Outputs:
- input_grads: bfloat16 [4096, 2048], P(('groups', 'expert', 'dp')), parts along dimension 0
- gate_grads: bfloat16 [4096, 8], P(('groups', 'expert', 'dp')), parts along dimension 0
- gate_weight_grads: bfloat16 [32, 2048, 384], P(('groups', 'expert'), 'dp'), parts along dimension 0
- up_weight_grads: bfloat16 [32, 2048, 384], P(('groups', 'expert'), 'dp'), parts along dimension 0
- down_weight_grads: bfloat16 [32, 384, 2048], P(('groups', 'expert'), None, 'dp'), parts along dimension 0
The draws below stay inside these ranges and needn't reach their ends.
There are 2 independent parts, one for each index of `groups`. The reference program is written for one: setup_inputs(seed, part) draws one part's arguments, and reference() takes and returns one part's arrays. A program takes and returns all parts, laid end to end along the dimension named above; an argument that names none is the same for every part. Nothing has to cross between parts.
Inputs may be any that keep to these rules, and one draw needn't show every extreme that they name: `routes`: each row names 8 different experts; among the rows of one device no expert is named more than 72 times, and in every draw some expert is named exactly 72 times by the rows of some device.
All inputs are finite; a program needn't handle non-finite values.
Results may differ from the reference program's by a relative error of at most 0.012.
Values may be sent and summed in bfloat16 or wider, within the bound.
A program may use at most 128 MiB of HBM per device.

```python
import math
import jax
import jax.numpy as jnp
import numpy as np
from jax import lax

D = 2048
FF = 384
TOP = 8
TOK_DEV = 128
EXPERTS = 16
TOKENS = 2048
CAP = 72
N_EXPERT = 8
N_DP = 2


def levels(own_key, extent, cuts, least, largest):
    loudness = 1.0
    for axis_at, blocks in cuts:
        draws = jax.random.uniform(jax.random.fold_in(jax.random.fold_in(own_key, 6), axis_at), (blocks,), jnp.float32, least / len(cuts), largest / len(cuts))
        loudness = loudness * jnp.repeat(jnp.exp(draws), extent[axis_at] // blocks).reshape((-1,) + (1,) * (len(extent) - 1 - axis_at))
    return loudness


def assign_block(stream_key, own, number, rows, amount, top, reach, skew):
    order = jax.random.permutation(stream_key, amount)
    heavy_load, ordinary = portions_of(amount, rows * top, reach, skew, True), portions_of(amount, rows * top, reach, skew, False)
    places = jnp.arange(amount)

    def named(lengths, offset_by):
        used = int((lengths > 0).sum())
        fixed = max(1, used // 4)
        moved = fixed + (places - fixed + offset_by * (used - fixed)) % max(1, amount - fixed)
        return jnp.zeros((amount,), jnp.int32).at[order[jnp.where(places < fixed, places, moved)]].set(jnp.asarray(lengths, jnp.int32))

    lengths = jnp.where(number % 4 == 0, named(heavy_load, number // 4), named(ordinary, number - number // 4 - 1))
    mixed = jax.random.permutation(jax.random.fold_in(own, 3), amount)
    donor, sink = mixed[0:amount // 2 * 2:2], mixed[1:amount // 2 * 2:2]
    room = jnp.minimum(lengths[donor] - 1, reach - lengths[sink]) // 2
    room = jnp.where((donor == order[0]) | (sink == order[0]) | (lengths[sink] == 0), 0, jnp.maximum(room, 0))
    moved = jax.random.randint(jax.random.fold_in(own, 4), (amount // 2,), 0, 1 << 20) % (room + 1)
    lengths = lengths.at[donor].add(-moved).at[sink].add(moved)
    items = jnp.searchsorted(jnp.cumsum(lengths), jnp.arange(rows * top), side="right").astype(jnp.int32)
    listing = items.reshape(top, rows).T
    listing = listing[jax.random.permutation(jax.random.fold_in(own, 1), rows)]
    offset_by = jax.random.randint(jax.random.fold_in(own, 2), (rows, 1), 0, top)
    return jnp.take_along_axis(listing, (jnp.arange(top)[None, :] + offset_by) % top, axis=1)


def portions_of(count, total, limit, lean, full):
    weights = [(1 << 20) // math.isqrt(rank ** lean) + 1 for rank in range(1, count + 1)]
    largest = limit if full else min(limit, max(-(-total // count), total * weights[0] // sum(weights)))
    least = 1 if total - largest >= count - 1 else 0
    given, surplus = [largest] + [least] * (count - 1), total - largest - least * (count - 1)
    while surplus > 0:
        candidates = [i for i in range(1, count) if given[i] < largest] or [i for i in range(1, count) if given[i] < limit]
        whole, budget = sum([weights[i] for i in candidates]), surplus
        for i in candidates:
            addition = min(limit - given[i], max(1, budget * weights[i] // whole), surplus)
            given[i] = given[i] + addition
            surplus = surplus - addition
    return np.array(given)


def scatter_about(stream_key, shape, scale, bound, split=(), kind=jnp.bfloat16):
    factor_of = levels(stream_key, shape, split, -0.22, 0.18) if split else 1.0
    array = jax.random.normal(stream_key, shape, jnp.float32) * scale * factor_of
    return jnp.minimum(jnp.maximum(array, -bound), bound).astype(kind)


def setup_inputs(seed: int = 0, part: int = 0) -> dict:
    arg_keys = jax.random.split(jax.random.key(seed), 8)
    part_splits = jax.random.split(jax.random.fold_in(arg_keys[7], part), 8)
    tokens = scatter_about(part_splits[0], (TOKENS, D), 1.0, 6.0, ((0, 16),))
    out_grads = scatter_about(part_splits[1], (TOKENS, D), 0.5, 3.0, ((0, 16),))
    routes_keys = jax.random.split(jax.random.fold_in(part_splits[2], 1), TOKENS // TOK_DEV)
    routes_turns = jax.random.permutation(jax.random.fold_in(part_splits[2], 3), TOKENS // TOK_DEV)
    routes = jax.vmap(lambda own, number: assign_block(jax.random.fold_in(part_splits[2], 2), own, number, TOK_DEV, EXPERTS, TOP, CAP, 1))(routes_keys, routes_turns).reshape((TOKENS, TOP))
    gates = jnp.clip(jnp.exp(math.log(0.5) - 2.306499 * jax.random.uniform(part_splits[3], (TOKENS, TOP), jnp.float32) ** levels(part_splits[3], (TOKENS, TOP), ((0, 16),), -0.2, 0.2)), 0.049804688, 0.5).astype(jnp.bfloat16)
    gate_weight = scatter_about(arg_keys[4], (EXPERTS, D, FF), D ** -0.5, 0.125, ((0, 8),))
    up_weight = scatter_about(arg_keys[5], (EXPERTS, D, FF), D ** -0.5, 0.125, ((0, 8),))
    down_weight = scatter_about(arg_keys[6], (EXPERTS, FF, D), FF ** -0.5, 0.3125, ((0, 8),))
    return {"tokens": tokens, "out_grads": out_grads, "routes": routes, "gates": gates, "gate_weight": gate_weight, "up_weight": up_weight, "down_weight": down_weight}


def reference(tokens, out_grads, routes, gates, gate_weight, up_weight, down_weight):
    blocks = TOKENS // TOK_DEV
    per_block = TOK_DEV * TOP
    flat_routes = routes.reshape(blocks, per_block)
    onehot = (flat_routes[:, :, None] == jnp.arange(EXPERTS, dtype=jnp.int32)[None, None, :]).astype(jnp.int32)
    positions = jnp.sum((jnp.cumsum(onehot, axis=1) - 1) * onehot, axis=2).astype(jnp.int32)
    slot_index = (flat_routes * CAP + positions).astype(jnp.int32)
    block_rows = jnp.arange(blocks, dtype=jnp.int32)[:, None]
    filler = jnp.broadcast_to(jnp.arange(per_block, dtype=jnp.int32)[None, :], (blocks, per_block))
    slot_table = jnp.full((blocks, EXPERTS * CAP), per_block, jnp.int32).at[block_rows, slot_index].set(filler)
    per_expert = jnp.transpose(slot_table.reshape(blocks, EXPERTS, CAP), (1, 0, 2))
    padded_x = jnp.concatenate([tokens, jnp.zeros((1, D), tokens.dtype)], axis=0)
    padded_dy = jnp.concatenate([out_grads, jnp.zeros((1, D), out_grads.dtype)], axis=0)
    padded_gate = jnp.concatenate([gates.reshape(-1), jnp.zeros((1,), gates.dtype)], axis=0)

    def one_expert(carry, inputs):
        grad_acc, route_acc = carry
        route_ids, w_gate, w_up, w_down = inputs
        valid = route_ids < per_block
        token_ids = jnp.where(valid, block_rows * TOK_DEV + route_ids // TOP, TOKENS).reshape(-1).astype(jnp.int32)
        route_rows = jnp.where(valid, block_rows * per_block + route_ids, TOKENS * TOP).reshape(-1).astype(jnp.int32)
        rows_x = padded_x[token_ids]
        rows_dy = padded_dy[token_ids]
        gate_col = padded_gate[route_rows].astype(jnp.float32)[:, None]
        pre_gate = jnp.dot(rows_x, w_gate, preferred_element_type=jnp.float32)
        pre_up = jnp.dot(rows_x, w_up, preferred_element_type=jnp.float32)
        sigmoid_gate = jax.nn.sigmoid(pre_gate)
        activated = pre_gate * sigmoid_gate
        hidden = activated * pre_up
        gated_hidden = (gate_col * hidden).astype(jnp.bfloat16)
        back_raw = jnp.dot(rows_dy, jnp.transpose(w_down), preferred_element_type=jnp.float32)
        route_grad = jnp.sum(hidden * back_raw, axis=-1).astype(jnp.bfloat16)
        back = gate_col * back_raw
        grad_gate = (back * pre_up * sigmoid_gate * (1.0 + pre_gate * (1.0 - sigmoid_gate))).astype(jnp.bfloat16)
        grad_up = (back * activated).astype(jnp.bfloat16)
        row_grads = (jnp.dot(grad_gate, jnp.transpose(w_gate), preferred_element_type=jnp.float32)
                     + jnp.dot(grad_up, jnp.transpose(w_up), preferred_element_type=jnp.float32)).astype(jnp.bfloat16)
        row_grads = lax.optimization_barrier(row_grads)
        route_grad = lax.optimization_barrier(route_grad)
        grad_acc = grad_acc.at[token_ids].add(row_grads.astype(jnp.float32))
        route_acc = route_acc.at[route_rows].set(route_grad.astype(jnp.float32))
        shape_rows = (N_EXPERT, N_DP, CAP)
        x_four = rows_x.astype(jnp.float32).reshape(shape_rows + (D,))
        dy_four = rows_dy.astype(jnp.float32).reshape(shape_rows + (D,))
        gate_four = grad_gate.astype(jnp.float32).reshape(shape_rows + (FF,))
        up_four = grad_up.astype(jnp.float32).reshape(shape_rows + (FF,))
        hidden_four = gated_hidden.astype(jnp.float32).reshape(shape_rows + (FF,))
        partial_gate = lax.optimization_barrier(jnp.einsum("epcd,epcf->pdf", x_four, gate_four).astype(jnp.bfloat16))
        partial_up = lax.optimization_barrier(jnp.einsum("epcd,epcf->pdf", x_four, up_four).astype(jnp.bfloat16))
        partial_down = lax.optimization_barrier(jnp.einsum("epcf,epcd->pfd", hidden_four, dy_four).astype(jnp.bfloat16))
        gate_sum = jnp.sum(partial_gate.astype(jnp.float32), axis=0).astype(jnp.bfloat16)
        up_sum = jnp.sum(partial_up.astype(jnp.float32), axis=0).astype(jnp.bfloat16)
        down_sum = jnp.sum(partial_down.astype(jnp.float32), axis=0).astype(jnp.bfloat16)
        return (grad_acc, route_acc), (gate_sum, up_sum, down_sum)

    start = (jnp.zeros((TOKENS + 1, D), jnp.float32), jnp.zeros((TOKENS * TOP + 1,), jnp.float32))
    (grad_acc, route_acc), (gate_grads_w, up_grads_w, down_grads_w) = lax.scan(
        one_expert, start, (per_expert, gate_weight, up_weight, down_weight))
    input_grads = grad_acc[:TOKENS].astype(jnp.bfloat16)
    gate_grads = route_acc[:TOKENS * TOP].reshape(TOKENS, TOP).astype(jnp.bfloat16)
    return (input_grads, gate_grads, gate_grads_w, up_grads_w, down_grads_w)
```

```python
import jax
import jax.numpy as jnp
from jax import lax
from jax.sharding import PartitionSpec as P

BF = jnp.bfloat16
F32 = jnp.float32


def per_device(tokens, out_grads, routes, gates, gate_weight, up_weight, down_weight):
    tok_rows, width = tokens.shape
    top = routes.shape[1]
    local = gate_weight.shape[0]
    groups = lax.axis_size("expert")
    experts = local * groups
    cap = min(tok_rows, max(2, (tok_rows * top * 9 + experts * 8 - 1) // (experts * 8)))
    me = lax.axis_index("expert")

    names = jnp.arange(experts, dtype=jnp.int32)
    hit = routes[:, :, None] == names[None, None, :]
    gate_map = jnp.sum(jnp.where(hit, gates[:, :, None].astype(F32), 0.0), axis=1).astype(BF)

    all_map = lax.all_gather(gate_map, "expert", axis=0)
    all_x = lax.all_gather(tokens, "expert", axis=0)
    all_dy = lax.all_gather(out_grads, "expert", axis=0)

    mine = lax.dynamic_slice_in_dim(all_map, me * local, local, axis=2).transpose(2, 0, 1)
    used = mine > 0
    tri = jnp.triu(jnp.ones((tok_rows, tok_rows), BF))
    place = jnp.dot(used.astype(BF).reshape(-1, tok_rows), tri, preferred_element_type=F32)
    place = place.astype(jnp.int32).reshape(used.shape) - 1
    pick = (place[:, :, None, :] == jnp.arange(cap, dtype=jnp.int32)[None, None, :, None]) & used[:, :, None, :]
    pick = pick.astype(BF)
    gate_col = jnp.einsum("lsct,lst->lsc", pick, mine, preferred_element_type=F32)
    gate_col = gate_col.reshape(local, -1, 1)
    rows_x = jnp.einsum("lsct,std->lscd", pick, all_x, preferred_element_type=F32).astype(BF)
    rows_x = rows_x.reshape(local, groups * cap, width)
    pre_gate = jnp.einsum("lcd,ldf->lcf", rows_x, gate_weight, preferred_element_type=F32)
    pre_up = jnp.einsum("lcd,ldf->lcf", rows_x, up_weight, preferred_element_type=F32)
    sig = jax.nn.sigmoid(pre_gate)
    act = pre_gate * sig
    hidden = act * pre_up
    gated_hidden = (gate_col * hidden).astype(BF)
    rows_dy = jnp.einsum("lsct,std->lscd", pick, all_dy, preferred_element_type=F32).astype(BF)
    rows_dy = rows_dy.reshape(local, groups * cap, width)
    down_part = jnp.einsum("lcf,lcd->lfd", gated_hidden, rows_dy, preferred_element_type=F32).astype(BF)
    down_sum = lax.psum_scatter(down_part, "dp", scatter_dimension=2, tiled=True)
    back_raw = jnp.einsum("lcd,lfd->lcf", rows_dy, down_weight, preferred_element_type=F32)
    route_grad = jnp.sum(hidden * back_raw, axis=-1).astype(BF)
    back = gate_col * back_raw
    grad_gate = (back * pre_up * sig * (1.0 + pre_gate * (1.0 - sig))).astype(BF)
    grad_up = (back * act).astype(BF)
    gate_part = jnp.einsum("lcd,lcf->ldf", rows_x, grad_gate, preferred_element_type=F32).astype(BF)
    gate_sum = lax.psum_scatter(gate_part, "dp", scatter_dimension=1, tiled=True)
    up_part = jnp.einsum("lcd,lcf->ldf", rows_x, grad_up, preferred_element_type=F32).astype(BF)
    up_sum = lax.psum_scatter(up_part, "dp", scatter_dimension=1, tiled=True)

    row_grads = (
        jnp.einsum("lcf,ldf->lcd", grad_gate, gate_weight, preferred_element_type=F32)
        + jnp.einsum("lcf,ldf->lcd", grad_up, up_weight, preferred_element_type=F32)
    ).astype(BF).reshape(local, groups, cap, width)
    token_part = jnp.einsum("lsct,lscd->std", pick, row_grads, preferred_element_type=F32).astype(BF)
    input_grads = lax.psum_scatter(token_part, "expert", scatter_dimension=0, tiled=True)[0]

    back_route = jnp.einsum(
        "lsct,lsc->slt", pick, route_grad.reshape(local, groups, cap), preferred_element_type=F32
    ).astype(BF)
    own_route = lax.all_to_all(back_route, "expert", split_axis=0, concat_axis=0, tiled=True)
    own_route = own_route.reshape(experts, tok_rows).T.astype(F32)
    gate_grads = jnp.sum(jnp.where(hit, own_route[:, None, :], 0.0), axis=2).astype(BF)
    return (input_grads, gate_grads, gate_sum, up_sum, down_sum)


def solution(mesh):
    rows = P(("groups", "expert", "dp"), None)
    in_specs = (rows, rows, rows, rows, P("expert", None, None), P("expert", None, None), P("expert", None, None))
    out_specs = (
        rows,
        rows,
        P(("groups", "expert"), "dp", None),
        P(("groups", "expert"), "dp", None),
        P(("groups", "expert"), None, "dp"),
    )
    return jax.shard_map(per_device, mesh=mesh, in_specs=in_specs, out_specs=out_specs, check_vma=False)
```

```python
import jax
import jax.numpy as jnp
from jax import lax
from jax.sharding import PartitionSpec as P

BF = jnp.bfloat16
F32 = jnp.float32


def halves(rows):
    if lax.axis_size("dp") != 2:
        return rows, rows
    at, width = lax.axis_index("dp"), rows.shape[-1] // 2
    return (
        lax.dynamic_slice_in_dim(rows, (1 - at) * width, width, axis=-1),
        lax.dynamic_slice_in_dim(rows, at * width, width, axis=-1),
    )


def replica_sum(grad, give, keep, dim):
    if lax.axis_size("dp") != 2:
        return lax.psum_scatter(grad(keep).astype(BF), "dp", scatter_dimension=dim, tiled=True)
    other = lax.ppermute(grad(give).astype(BF), "dp", [(0, 1), (1, 0)])
    own = grad(keep).astype(BF)
    return (own.astype(F32) + other.astype(F32)).astype(BF)


def per_device(tokens, out_grads, routes, gates, gate_weight, up_weight, down_weight):
    tok_rows, width = tokens.shape
    top = routes.shape[1]
    local = gate_weight.shape[0]
    groups = lax.axis_size("expert")
    experts = local * groups
    cap = min(tok_rows, max(2, (tok_rows * top * 9 + experts * 8 - 1) // (experts * 8)))
    me = lax.axis_index("expert")

    names = jnp.arange(experts, dtype=jnp.int32)
    hit = routes[:, :, None] == names[None, None, :]
    gate_map = jnp.sum(jnp.where(hit, gates[:, :, None].astype(F32), 0.0), axis=1).astype(BF)

    all_map = lax.all_gather(gate_map, "expert", axis=0)
    all_x = lax.all_gather(tokens, "expert", axis=0)
    all_dy = lax.all_gather(out_grads, "expert", axis=0)

    mine = lax.dynamic_slice_in_dim(all_map, me * local, local, axis=2).transpose(2, 0, 1)
    used = mine > 0
    tri = jnp.triu(jnp.ones((tok_rows, tok_rows), BF))
    place = jnp.dot(used.astype(BF).reshape(-1, tok_rows), tri, preferred_element_type=F32)
    place = place.astype(jnp.int32).reshape(used.shape) - 1
    pick = (place[:, :, None, :] == jnp.arange(cap, dtype=jnp.int32)[None, None, :, None]) & used[:, :, None, :]
    pick = pick.astype(BF)
    gate_col = jnp.einsum("lsct,lst->lsc", pick, mine, preferred_element_type=F32)
    gate_col = gate_col.reshape(local, -1, 1)
    rows_x = jnp.einsum("lsct,std->lscd", pick, all_x, preferred_element_type=F32).astype(BF)
    rows_x = rows_x.reshape(local, groups * cap, width)
    pre_gate = jnp.einsum("lcd,ldf->lcf", rows_x, gate_weight, preferred_element_type=F32)
    pre_up = jnp.einsum("lcd,ldf->lcf", rows_x, up_weight, preferred_element_type=F32)
    sig = jax.nn.sigmoid(pre_gate)
    act = pre_gate * sig
    hidden = act * pre_up
    gated_hidden = (gate_col * hidden).astype(BF)
    rows_dy = jnp.einsum("lsct,std->lscd", pick, all_dy, preferred_element_type=F32).astype(BF)
    rows_dy = rows_dy.reshape(local, groups * cap, width)
    give_dy, keep_dy = halves(rows_dy)
    down_sum = replica_sum(lambda d: jnp.einsum("lcf,lcd->lfd", gated_hidden, d, preferred_element_type=F32), give_dy, keep_dy, 2)
    back_raw = jnp.einsum("lcd,lfd->lcf", rows_dy, down_weight, preferred_element_type=F32)
    route_grad = jnp.sum(hidden * back_raw, axis=-1).astype(BF)
    back = gate_col * back_raw
    grad_gate = (back * pre_up * sig * (1.0 + pre_gate * (1.0 - sig))).astype(BF)
    grad_up = (back * act).astype(BF)
    give_x, keep_x = halves(rows_x)
    gate_sum = replica_sum(lambda d: jnp.einsum("lcd,lcf->ldf", d, grad_gate, preferred_element_type=F32), give_x, keep_x, 1)
    up_sum = replica_sum(lambda d: jnp.einsum("lcd,lcf->ldf", d, grad_up, preferred_element_type=F32), give_x, keep_x, 1)

    row_grads = (
        jnp.einsum("lcf,ldf->lcd", grad_gate, gate_weight, preferred_element_type=F32)
        + jnp.einsum("lcf,ldf->lcd", grad_up, up_weight, preferred_element_type=F32)
    ).astype(BF).reshape(local, groups, cap, width)
    token_part = jnp.einsum("lsct,lscd->std", pick, row_grads, preferred_element_type=F32).astype(BF)
    input_grads = lax.psum_scatter(token_part, "expert", scatter_dimension=0, tiled=True)[0]

    back_route = jnp.einsum(
        "lsct,lsc->slt", pick, route_grad.reshape(local, groups, cap), preferred_element_type=F32
    ).astype(BF)
    own_route = lax.all_to_all(back_route, "expert", split_axis=0, concat_axis=0, tiled=True)
    own_route = own_route.reshape(experts, tok_rows).T.astype(F32)
    gate_grads = jnp.sum(jnp.where(hit, own_route[:, None, :], 0.0), axis=2).astype(BF)
    return (input_grads, gate_grads, gate_sum, up_sum, down_sum)


def solution(mesh):
    rows = P(("groups", "expert", "dp"), None)
    in_specs = (rows, rows, rows, rows, P("expert", None, None), P("expert", None, None), P("expert", None, None))
    out_specs = (
        rows,
        rows,
        P(("groups", "expert"), "dp", None),
        P(("groups", "expert"), "dp", None),
        P(("groups", "expert"), None, "dp"),
    )
    return jax.shard_map(per_device, mesh=mesh, in_specs=in_specs, out_specs=out_specs, check_vma=False)
```

```python
import functools

import jax
import jax.numpy as jnp
from jax import lax
from jax.experimental import pallas as pl
from jax.experimental.pallas import tpu as pltpu
from jax.sharding import PartitionSpec as P

BF = jnp.bfloat16
F32 = jnp.float32


def gather_kernel(chips, count, *refs):
    ins, outs = refs[:count], refs[count : 2 * count]
    local_sem, up_sem, down_sem, side_sem, line_recv, side_recv = refs[2 * count :]
    me = lax.axis_index("expert")
    chip, core = me // 2, me % 2
    side = chip * 2 + 1 - core
    above, below = me + 2, me - 2
    has_above, has_below = chip < chips - 1, chip > 0

    barrier = pltpu.get_barrier_semaphore()
    pl.semaphore_signal(barrier, inc=1, device_id={"expert": side}, device_id_type=pl.DeviceIdType.MESH)

    @pl.when(has_above)
    def _():
        pl.semaphore_signal(barrier, inc=1, device_id={"expert": above}, device_id_type=pl.DeviceIdType.MESH)

    @pl.when(has_below)
    def _():
        pl.semaphore_signal(barrier, inc=1, device_id={"expert": below}, device_id_type=pl.DeviceIdType.MESH)

    peers = 1 + jnp.where(has_above, 1, 0) + jnp.where(has_below, 1, 0)
    pl.semaphore_wait(barrier, peers)

    def copy(which, src, origin, sems, recvs, target, from_core):
        return pltpu.make_async_remote_copy(
            src_ref=src,
            dst_ref=outs[which].at[origin * 2 + from_core],
            send_sem=sems.at[origin, which],
            recv_sem=recvs.at[origin, which],
            device_id={"expert": target},
            device_id_type=pl.DeviceIdType.MESH,
        )

    def up(which, src, origin):
        return copy(which, src, origin, up_sem, line_recv, above, core)

    def down(which, src, origin):
        return copy(which, src, origin, down_sem, line_recv, below, core)

    def across(which, src, origin):
        return copy(which, src, origin, side_sem, side_recv, side, core)

    def own(which):
        return pltpu.make_async_copy(ins[which], outs[which].at[me], local_sem.at[which])

    for which in range(count):
        pl.when(has_above)(lambda w=which: up(w, ins[w], chip).start())
        pl.when(has_below)(lambda w=which: down(w, ins[w], chip).start())
    for which in range(count):
        across(which, ins[which], chip).start()
        own(which).start()

    for far in range(1, chips):
        for which in range(count):

            @pl.when(chip - far >= 0)
            def _(which=which, origin=chip - far):
                block = outs[which].at[origin * 2 + core]
                up(which, block, origin).wait_recv()
                pl.when(has_above)(lambda: up(which, block, origin).start())
                across(which, block, origin).start()

            @pl.when(chip + far < chips)
            def _(which=which, origin=chip + far):
                block = outs[which].at[origin * 2 + core]
                down(which, block, origin).wait_recv()
                pl.when(has_below)(lambda: down(which, block, origin).start())
                across(which, block, origin).start()

    for which in range(count):
        own(which).wait()
        for origin in range(chips):
            block = outs[which].at[origin * 2 + core]
            across(which, block, origin).wait_send()
            copy(which, block, origin, side_sem, side_recv, side, 1 - core).wait_recv()
            pl.when(has_above & (origin <= chip))(lambda w=which, b=block, o=origin: up(w, b, o).wait_send())
            pl.when(has_below & (origin >= chip))(lambda w=which, b=block, o=origin: down(w, b, o).wait_send())


def gather(*arrays):
    n = lax.axis_size("expert")
    chips, count = n // 2, len(arrays)
    size = sum(a.size * a.dtype.itemsize for a in arrays)
    return pl.pallas_call(
        functools.partial(gather_kernel, chips, count),
        out_shape=[jax.ShapeDtypeStruct((n,) + a.shape, a.dtype) for a in arrays],
        in_specs=[pl.BlockSpec(memory_space=pl.ANY)] * count,
        out_specs=[pl.BlockSpec(memory_space=pl.ANY)] * count,
        scratch_shapes=[pltpu.SemaphoreType.DMA((count,))] + [pltpu.SemaphoreType.DMA((chips, count))] * 5,
        compiler_params=pltpu.CompilerParams(collective_id=0, has_side_effects=True),
        cost_estimate=pl.CostEstimate(flops=0, bytes_accessed=2 * n * size, transcendentals=0),
        name="gather_line",
    )(*arrays)


def halves(rows):
    if lax.axis_size("dp") != 2:
        return rows, rows
    at, width = lax.axis_index("dp"), rows.shape[-1] // 2
    return (
        lax.dynamic_slice_in_dim(rows, (1 - at) * width, width, axis=-1),
        lax.dynamic_slice_in_dim(rows, at * width, width, axis=-1),
    )


def replica_sum(grad, give, keep, dim):
    if lax.axis_size("dp") != 2:
        return lax.psum_scatter(grad(keep).astype(BF), "dp", scatter_dimension=dim, tiled=True)
    other = lax.ppermute(grad(give).astype(BF), "dp", [(0, 1), (1, 0)])
    own = grad(keep).astype(BF)
    return (own.astype(F32) + other.astype(F32)).astype(BF)


def per_device(tokens, out_grads, routes, gates, gate_weight, up_weight, down_weight):
    tok_rows, width = tokens.shape
    top = routes.shape[1]
    local = gate_weight.shape[0]
    groups = lax.axis_size("expert")
    experts = local * groups
    cap = min(tok_rows, max(2, (tok_rows * top * 9 + experts * 8 - 1) // (experts * 8)))
    me = lax.axis_index("expert")

    names = jnp.arange(experts, dtype=jnp.int32)
    hit = routes[:, :, None] == names[None, None, :]
    gate_map = jnp.sum(jnp.where(hit, gates[:, :, None].astype(F32), 0.0), axis=1).astype(BF)

    pad = -experts % 128
    all_x, all_dy, all_map = gather(tokens, out_grads, jnp.pad(gate_map, ((0, 0), (0, pad))))

    mine = lax.dynamic_slice_in_dim(all_map, me * local, local, axis=2).transpose(2, 0, 1)
    used = mine > 0
    tri = jnp.triu(jnp.ones((tok_rows, tok_rows), BF))
    place = jnp.dot(used.astype(BF).reshape(-1, tok_rows), tri, preferred_element_type=F32)
    place = place.astype(jnp.int32).reshape(used.shape) - 1
    pick = (place[:, :, None, :] == jnp.arange(cap, dtype=jnp.int32)[None, None, :, None]) & used[:, :, None, :]
    pick = pick.astype(BF)
    gate_col = jnp.einsum("lsct,lst->lsc", pick, mine, preferred_element_type=F32)
    gate_col = gate_col.reshape(local, -1, 1)
    rows_x = jnp.einsum("lsct,std->lscd", pick, all_x, preferred_element_type=F32).astype(BF)
    rows_x = rows_x.reshape(local, groups * cap, width)
    pre_gate = jnp.einsum("lcd,ldf->lcf", rows_x, gate_weight, preferred_element_type=F32)
    pre_up = jnp.einsum("lcd,ldf->lcf", rows_x, up_weight, preferred_element_type=F32)
    sig = jax.nn.sigmoid(pre_gate)
    act = pre_gate * sig
    hidden = act * pre_up
    gated_hidden = (gate_col * hidden).astype(BF)
    rows_dy = jnp.einsum("lsct,std->lscd", pick, all_dy, preferred_element_type=F32).astype(BF)
    rows_dy = rows_dy.reshape(local, groups * cap, width)
    give_dy, keep_dy = halves(rows_dy)
    down_sum = replica_sum(lambda d: jnp.einsum("lcf,lcd->lfd", gated_hidden, d, preferred_element_type=F32), give_dy, keep_dy, 2)
    back_raw = jnp.einsum("lcd,lfd->lcf", rows_dy, down_weight, preferred_element_type=F32)
    route_grad = jnp.sum(hidden * back_raw, axis=-1).astype(BF)
    back = gate_col * back_raw
    grad_gate = (back * pre_up * sig * (1.0 + pre_gate * (1.0 - sig))).astype(BF)
    grad_up = (back * act).astype(BF)
    give_x, keep_x = halves(rows_x)
    gate_sum = replica_sum(lambda d: jnp.einsum("lcd,lcf->ldf", d, grad_gate, preferred_element_type=F32), give_x, keep_x, 1)
    up_sum = replica_sum(lambda d: jnp.einsum("lcd,lcf->ldf", d, grad_up, preferred_element_type=F32), give_x, keep_x, 1)

    row_grads = (
        jnp.einsum("lcf,ldf->lcd", grad_gate, gate_weight, preferred_element_type=F32)
        + jnp.einsum("lcf,ldf->lcd", grad_up, up_weight, preferred_element_type=F32)
    ).astype(BF).reshape(local, groups, cap, width)
    token_part = jnp.einsum("lsct,lscd->std", pick, row_grads, preferred_element_type=F32).astype(BF)
    input_grads = lax.psum_scatter(token_part, "expert", scatter_dimension=0, tiled=True)[0]

    back_route = jnp.einsum(
        "lsct,lsc->slt", pick, route_grad.reshape(local, groups, cap), preferred_element_type=F32
    ).astype(BF)
    own_route = lax.all_to_all(back_route, "expert", split_axis=0, concat_axis=0, tiled=True)
    own_route = own_route.reshape(experts, tok_rows).T.astype(F32)
    gate_grads = jnp.sum(jnp.where(hit, own_route[:, None, :], 0.0), axis=2).astype(BF)
    return (input_grads, gate_grads, gate_sum, up_sum, down_sum)


def solution(mesh):
    rows = P(("groups", "expert", "dp"), None)
    in_specs = (rows, rows, rows, rows, P("expert", None, None), P("expert", None, None), P("expert", None, None))
    out_specs = (
        rows,
        rows,
        P(("groups", "expert"), "dp", None),
        P(("groups", "expert"), "dp", None),
        P(("groups", "expert"), None, "dp"),
    )
    return jax.shard_map(per_device, mesh=mesh, in_specs=in_specs, out_specs=out_specs, check_vma=False)
```

```python
import functools

import jax
import jax.numpy as jnp
from jax import lax
from jax.experimental import pallas as pl
from jax.experimental.pallas import tpu as pltpu
from jax.sharding import PartitionSpec as P

BF = jnp.bfloat16
F32 = jnp.float32


def gather_kernel(chips, count, *refs):
    ins, outs = refs[:count], refs[count : 2 * count]
    local_sem, up_sem, down_sem, side_sem, line_recv, side_recv = refs[2 * count :]
    me = lax.axis_index("expert")
    chip, core = me // 2, me % 2
    side = chip * 2 + 1 - core
    above, below = me + 2, me - 2
    has_above, has_below = chip < chips - 1, chip > 0

    barrier = pltpu.get_barrier_semaphore()
    pl.semaphore_signal(barrier, inc=1, device_id={"expert": side}, device_id_type=pl.DeviceIdType.MESH)

    @pl.when(has_above)
    def _():
        pl.semaphore_signal(barrier, inc=1, device_id={"expert": above}, device_id_type=pl.DeviceIdType.MESH)

    @pl.when(has_below)
    def _():
        pl.semaphore_signal(barrier, inc=1, device_id={"expert": below}, device_id_type=pl.DeviceIdType.MESH)

    peers = 1 + jnp.where(has_above, 1, 0) + jnp.where(has_below, 1, 0)
    pl.semaphore_wait(barrier, peers)

    def copy(which, src, origin, sems, recvs, target, from_core):
        return pltpu.make_async_remote_copy(
            src_ref=src,
            dst_ref=outs[which].at[origin * 2 + from_core],
            send_sem=sems.at[origin, which],
            recv_sem=recvs.at[origin, which],
            device_id={"expert": target},
            device_id_type=pl.DeviceIdType.MESH,
        )

    def up(which, src, origin):
        return copy(which, src, origin, up_sem, line_recv, above, core)

    def down(which, src, origin):
        return copy(which, src, origin, down_sem, line_recv, below, core)

    def across(which, src, origin):
        return copy(which, src, origin, side_sem, side_recv, side, core)

    def own(which):
        return pltpu.make_async_copy(ins[which], outs[which].at[me], local_sem.at[which])

    for which in range(count):
        pl.when(has_above)(lambda w=which: up(w, ins[w], chip).start())
        pl.when(has_below)(lambda w=which: down(w, ins[w], chip).start())
    for which in range(count):
        across(which, ins[which], chip).start()
        own(which).start()

    for far in range(1, chips):
        for which in range(count):

            @pl.when(chip - far >= 0)
            def _(which=which, origin=chip - far):
                block = outs[which].at[origin * 2 + core]
                up(which, block, origin).wait_recv()
                pl.when(has_above)(lambda: up(which, block, origin).start())
                across(which, block, origin).start()

            @pl.when(chip + far < chips)
            def _(which=which, origin=chip + far):
                block = outs[which].at[origin * 2 + core]
                down(which, block, origin).wait_recv()
                pl.when(has_below)(lambda: down(which, block, origin).start())
                across(which, block, origin).start()

    for which in range(count):
        own(which).wait()
        for origin in range(chips):
            block = outs[which].at[origin * 2 + core]
            across(which, block, origin).wait_send()
            copy(which, block, origin, side_sem, side_recv, side, 1 - core).wait_recv()
            pl.when(has_above & (origin <= chip))(lambda w=which, b=block, o=origin: up(w, b, o).wait_send())
            pl.when(has_below & (origin >= chip))(lambda w=which, b=block, o=origin: down(w, b, o).wait_send())


def gather(*arrays):
    n = lax.axis_size("expert")
    chips, count = n // 2, len(arrays)
    size = sum(a.size * a.dtype.itemsize for a in arrays)
    return pl.pallas_call(
        functools.partial(gather_kernel, chips, count),
        out_shape=[jax.ShapeDtypeStruct((n,) + a.shape, a.dtype) for a in arrays],
        in_specs=[pl.BlockSpec(memory_space=pl.ANY)] * count,
        out_specs=[pl.BlockSpec(memory_space=pl.ANY)] * count,
        scratch_shapes=[pltpu.SemaphoreType.DMA((count,))] + [pltpu.SemaphoreType.DMA((chips, count))] * 5,
        compiler_params=pltpu.CompilerParams(collective_id=0, has_side_effects=True),
        cost_estimate=pl.CostEstimate(flops=0, bytes_accessed=2 * n * size, transcendentals=0),
        name="gather_line",
    )(*arrays)


SWAP = [(0, 1), (1, 0)]


def picks(gate, cap):
    used = gate > 0
    tok_rows = gate.shape[-1]
    tri = jnp.triu(jnp.ones((tok_rows, tok_rows), BF))
    place = jnp.dot(used.astype(BF).reshape(-1, tok_rows), tri, preferred_element_type=F32)
    place = place.astype(jnp.int32).reshape(used.shape) - 1
    slots = jnp.arange(cap, dtype=jnp.int32)[None, None, :, None]
    return ((place[:, :, None, :] == slots) & used[:, :, None, :]).astype(BF)


def halves(rows):
    if lax.axis_size("dp") != 2:
        return rows, rows
    at, width = lax.axis_index("dp"), rows.shape[-1] // 2
    return (
        lax.dynamic_slice_in_dim(rows, (1 - at) * width, width, axis=-1),
        lax.dynamic_slice_in_dim(rows, at * width, width, axis=-1),
    )


def replica_sum(grad, give, keep, dim):
    if lax.axis_size("dp") != 2:
        return lax.psum_scatter(grad(keep).astype(BF), "dp", scatter_dimension=dim, tiled=True)
    other = lax.ppermute(grad(give).astype(BF), "dp", SWAP)
    own = grad(keep).astype(BF)
    return (own.astype(F32) + other.astype(F32)).astype(BF)


def per_device(tokens, out_grads, routes, gates, gate_weight, up_weight, down_weight):
    tok_rows, width = tokens.shape
    top = routes.shape[1]
    local = gate_weight.shape[0]
    groups = lax.axis_size("expert")
    experts = local * groups
    cap = min(tok_rows, max(2, (tok_rows * top * 9 + experts * 8 - 1) // (experts * 8)))
    me = lax.axis_index("expert")

    names = jnp.arange(experts, dtype=jnp.int32)
    hit = routes[:, :, None] == names[None, None, :]
    gate_map = jnp.sum(jnp.where(hit, gates[:, :, None].astype(F32), 0.0), axis=1).astype(BF)

    paired = lax.axis_size("dp") == 2
    if paired:
        other_x = lax.ppermute(halves(tokens)[0], "dp", SWAP)
    pad = -experts % 128
    all_x, all_dy, all_map = gather(tokens, out_grads, jnp.pad(gate_map, ((0, 0), (0, pad))))

    mine = lax.dynamic_slice_in_dim(all_map, me * local, local, axis=2).transpose(2, 0, 1)
    pick = picks(mine, cap)
    if paired:
        other_pick = picks(lax.ppermute(mine, "dp", SWAP), cap)
        other_x, all_x = lax.optimization_barrier((other_x, all_x))
        other_x = lax.all_gather(other_x, "expert", axis=0)
        other_rows = jnp.einsum("lsct,std->lscd", other_pick, other_x, preferred_element_type=F32).astype(BF)
        other_rows = other_rows.reshape(local, groups * cap, width // 2)
    gate_col = jnp.einsum("lsct,lst->lsc", pick, mine, preferred_element_type=F32)
    gate_col = gate_col.reshape(local, -1, 1)
    rows_x = jnp.einsum("lsct,std->lscd", pick, all_x, preferred_element_type=F32).astype(BF)
    rows_x = rows_x.reshape(local, groups * cap, width)
    pre_gate = jnp.einsum("lcd,ldf->lcf", rows_x, gate_weight, preferred_element_type=F32)
    pre_up = jnp.einsum("lcd,ldf->lcf", rows_x, up_weight, preferred_element_type=F32)
    sig = jax.nn.sigmoid(pre_gate)
    act = pre_gate * sig
    hidden = act * pre_up
    gated_hidden = (gate_col * hidden).astype(BF)
    rows_dy = jnp.einsum("lsct,std->lscd", pick, all_dy, preferred_element_type=F32).astype(BF)
    rows_dy = rows_dy.reshape(local, groups * cap, width)
    back_raw = jnp.einsum("lcd,lfd->lcf", rows_dy, down_weight, preferred_element_type=F32)
    route_grad = jnp.sum(hidden * back_raw, axis=-1).astype(BF)
    back = gate_col * back_raw
    grad_gate = (back * pre_up * sig * (1.0 + pre_gate * (1.0 - sig))).astype(BF)
    grad_up = (back * act).astype(BF)
    if paired:
        gated_hidden, grad_gate, grad_up = lax.optimization_barrier((gated_hidden, grad_gate, grad_up))
        other_gate = lax.ppermute(grad_gate, "dp", SWAP)
        other_up = lax.ppermute(grad_up, "dp", SWAP)
    give_dy, keep_dy = halves(rows_dy)
    down_sum = replica_sum(lambda d: jnp.einsum("lcf,lcd->lfd", gated_hidden, d, preferred_element_type=F32), give_dy, keep_dy, 2)
    give_x, keep_x = halves(rows_x)

    def outer(rows, grads):
        return jnp.einsum("lcd,lcf->ldf", rows, grads, preferred_element_type=F32)

    if paired:
        own_gate = outer(keep_x, grad_gate).astype(BF)
        own_up = outer(keep_x, grad_up).astype(BF)
        gate_sum = (own_gate.astype(F32) + outer(other_rows, other_gate).astype(BF).astype(F32)).astype(BF)
        up_sum = (own_up.astype(F32) + outer(other_rows, other_up).astype(BF).astype(F32)).astype(BF)
    else:
        gate_sum = replica_sum(lambda d: outer(d, grad_gate), give_x, keep_x, 1)
        up_sum = replica_sum(lambda d: outer(d, grad_up), give_x, keep_x, 1)

    row_grads = (
        jnp.einsum("lcf,ldf->lcd", grad_gate, gate_weight, preferred_element_type=F32)
        + jnp.einsum("lcf,ldf->lcd", grad_up, up_weight, preferred_element_type=F32)
    ).astype(BF).reshape(local, groups, cap, width)
    token_part = jnp.einsum("lsct,lscd->std", pick, row_grads, preferred_element_type=F32).astype(BF)
    input_grads = lax.psum_scatter(token_part, "expert", scatter_dimension=0, tiled=True)[0]

    back_route = jnp.einsum(
        "lsct,lsc->slt", pick, route_grad.reshape(local, groups, cap), preferred_element_type=F32
    ).astype(BF)
    own_route = lax.all_to_all(back_route, "expert", split_axis=0, concat_axis=0, tiled=True)
    own_route = own_route.reshape(experts, tok_rows).T.astype(F32)
    gate_grads = jnp.sum(jnp.where(hit, own_route[:, None, :], 0.0), axis=2).astype(BF)
    return (input_grads, gate_grads, gate_sum, up_sum, down_sum)


def solution(mesh):
    rows = P(("groups", "expert", "dp"), None)
    in_specs = (rows, rows, rows, rows, P("expert", None, None), P("expert", None, None), P("expert", None, None))
    out_specs = (
        rows,
        rows,
        P(("groups", "expert"), "dp", None),
        P(("groups", "expert"), "dp", None),
        P(("groups", "expert"), None, "dp"),
    )
    return jax.shard_map(per_device, mesh=mesh, in_specs=in_specs, out_specs=out_specs, check_vma=False)
```
